32 devices in a mesh: groups: 2 (over y), dp: 4 (over x, core), mp: 4 (over z).
Axes of the slice: x: 2, y: 2, z: 4, core: 2. Of those that a mesh axis runs over, the one named last changes fastest.
Arguments:
- tokens: int32 [16, 512], P(('groups', 'dp')), parts along dimension 0, may hold values from 0 to 128255
- acts: bfloat16 [8192, 20480], P(('groups', 'dp'), 'mp'), parts along dimension 0, may hold values from -6 to 6
- resid: bfloat16 [8192, 8192], P(('groups', 'dp'), 'mp'), parts along dimension 0, may hold values from -6 to 6
- cotangent: bfloat16 [8192, 8192], P(('groups', 'dp'), 'mp'), parts along dimension 0, may hold values from -6 to 6
- weight: bfloat16 [20480, 8192], P('mp'), may hold values from -0.0625 to 0.0625
- gain: bfloat16 [8192], P('mp'), may hold values from 0.099609375 to 1.8984375
- proj_in: bfloat16 [20480, 64], P('mp'), may hold values from -0.0390625 to 0.0390625
- proj_out: bfloat16 [8192, 64], P('mp'), may hold values from -0.0625 to 0.0625
- tok_weight: float32 [128256], replicated, may hold values from 0.25 to 4
- lengths: int32 [16], P(('groups', 'dp')), parts along dimension 0, may hold values from 128 to 512, as said below
- queries: bfloat16 [4096, 4096], P('dp', 'mp'), may hold values from -0.0234375 to 0.0234375
- query_ids: int32 [4096], replicated, may hold values from 0 to 255
Outputs:
- stream: bfloat16 [8192, 8192], P(('groups', 'dp'), 'mp'), parts along dimension 0
- scores: float32 [16, 256], P(('groups', 'dp')), parts along dimension 0
The draws below stay inside these ranges and needn't reach their ends.
There are 2 independent parts, one for each index of `groups`. The reference program is written for one: setup_inputs(seed, part) draws one part's arguments, and reference() takes and returns one part's arrays. A program takes and returns all parts, laid end to end along the dimension named above; an argument that names none is the same for every part. Nothing has to cross between parts.
Inputs may be any that keep to these rules, and one draw needn't show every extreme that they name: `lengths`: document 0 has length 512.
All inputs are finite; a program needn't handle non-finite values.
Results may differ from the reference program's by a relative error of at most 0.015.
Values may be sent and summed in bfloat16 or wider, within the bound.
A program may use at most 320 MiB of HBM per device.

```python
import math
import jax
import jax.numpy as jnp
import numpy as np
from jax import lax

D = 8192
VOCAB = 128256
FF = 20480
R = 64
SEQ = 512
NQ = 4096
QG = 256
NF = 4096
DOCS = 8
TOKENS = 4096
N_MP = 4


def draw_lengths(key, part):
    key = jax.random.fold_in(key, 7)
    key_len, key_full = jax.random.split(key)
    drawn_len = jax.random.randint(key_len, (DOCS,), SEQ // 4, SEQ + 1, dtype=jnp.int32)
    full_pick = jax.random.randint(key_full, (DOCS,), 0, 2, dtype=jnp.int32)
    doc_lengths = jnp.where(full_pick == 1, jnp.int32(SEQ), drawn_len)
    return doc_lengths.at[0].set(SEQ).astype(jnp.int32)


def plant(array, key, least, high):
    longest = array.shape.index(max(array.shape))
    spots = []
    for shift in (0, 1):
        where = [jax.random.randint(jax.random.fold_in(key, axis), (), 0, length) for axis, length in enumerate(array.shape)]
        where[longest] = (where[longest] + shift) % array.shape[longest]
        spots.append(tuple(where))
    return array.at[spots[0]].set(least).at[spots[1]].set(high)


def with_spikes(array, rng, source, target, parts, factor):
    def block_of(axis_at):
        return (jnp.arange(array.shape[axis_at]) // (array.shape[axis_at] // parts)).reshape((-1,) + (1,) * (array.ndim - 1 - axis_at))

    first = jax.random.permutation(rng, parts)[block_of(target)]
    second = (block_of(target) + parts // 2) % parts
    return jnp.where((block_of(source) == first) | (block_of(source) == second), factor * array, array)


def levels(key, dims, shards, smallest, high):
    def one(axis_at, parts):
        steps = jax.random.uniform(jax.random.fold_in(jax.random.fold_in(key, 6), axis_at), (parts,), jnp.float32, smallest / len(shards), high / len(shards))
        return jnp.repeat(jnp.exp(steps), dims[axis_at] // parts).reshape((-1,) + (1,) * (len(dims) - axis_at - 1))

    loudness = one(*shards[0])
    for cut in shards[1:]:
        loudness = loudness * one(*cut)
    return loudness


def skewed_wide(rng, shape, amount, lean):
    loads = [min(1 << octave, amount + 1 - (1 << octave)) * (1 << 20) // math.isqrt((1 << octave) ** lean) + 1 for octave in range((amount + 1).bit_length()) if 1 << octave <= amount]
    scale = 1 + sum(loads) // (1 << 30)
    table = np.cumsum(np.array([max(1, weight // scale) for weight in loads]))
    ticket = jax.random.randint(jax.random.fold_in(rng, 1), shape, 0, int(table[len(loads) - 1]))
    start = jnp.left_shift(1, jnp.searchsorted(jnp.asarray(table, jnp.int32), ticket, side="right").astype(jnp.int32))
    standing = start - 1 + jax.random.randint(jax.random.fold_in(rng, 4), shape, 0, 1 << 30) % jnp.minimum(start, amount + 1 - start)
    return jax.random.permutation(jax.random.fold_in(rng, 2), amount)[standing].astype(jnp.int32)


def noise(own_key, shape, width, bound, pieces=(), held_as=jnp.bfloat16):
    factor_of = levels(own_key, shape, pieces, -0.22, 0.18) if pieces else 1.0
    values = jax.random.normal(own_key, shape, jnp.float32) * width * factor_of
    return jnp.minimum(jnp.maximum(values, -bound), bound).astype(held_as)


def noise_with(stream_key, shape, scale, limit, cuts, heavy, kind=jnp.bfloat16):
    drawn = scale * jax.random.normal(stream_key, shape, jnp.float32)
    if cuts:
        drawn = drawn * levels(stream_key, shape, cuts, -0.22, 0.18)
    return jnp.clip(with_spikes(drawn, jax.random.fold_in(stream_key, 3), *heavy), -limit, limit).astype(kind)


def setup_inputs(seed: int = 0, part: int = 0) -> dict:
    key_of = jax.random.split(jax.random.key(seed), 13)
    part_splits = jax.random.split(jax.random.fold_in(key_of[12], part), 13)
    tokens = plant(skewed_wide(part_splits[0], (DOCS, SEQ), VOCAB, 2), jax.random.fold_in(part_splits[0], 3), 0, VOCAB - 1).astype(jnp.int32)
    acts = noise(part_splits[1], (TOKENS, FF), 1.0, 6.0, ((0, 4), (1, 4)))
    resid = noise(part_splits[2], (TOKENS, D), 1.0, 6.0, ((0, 4), (1, 4)))
    cotangent = noise(part_splits[3], (TOKENS, D), 1.0, 6.0, ((0, 4), (1, 4)))
    weight = noise_with(key_of[4], (FF, D), FF ** -0.5, 0.0625, ((0, 4),), (0, 1, 4, 2.0))
    gain = jnp.clip(1.0 + 0.18 * jax.random.normal(key_of[5], (D,), jnp.float32), 0.099609375, 1.8984375).astype(jnp.bfloat16)
    proj_in = noise(key_of[6], (FF, R), FF ** -0.5, 0.0390625, ((0, 4),))
    proj_out = noise(key_of[7], (D, R), D ** -0.5, 0.0625, ((0, 4),))
    tok_weight = jnp.clip(jnp.exp(jax.random.uniform(key_of[8], (VOCAB,), jnp.float32, math.log(0.25), math.log(4.0))), 0.25, 4.0)
    lengths = draw_lengths(jax.random.fold_in(jax.random.fold_in(key_of[12], part), 71), part)
    queries = noise(key_of[10], (NQ, NF), (NF * NQ // QG) ** -0.5, 0.0234375, ((0, 4), (1, 4)))
    query_ids = plant(jax.random.randint(key_of[11], (NQ,), 0, QG), jax.random.fold_in(key_of[11], 1), 0, QG - 1).astype(jnp.int32)
    return {"tokens": tokens, "acts": acts, "resid": resid, "cotangent": cotangent, "weight": weight, "gain": gain, "proj_in": proj_in, "proj_out": proj_out, "tok_weight": tok_weight, "lengths": lengths, "queries": queries, "query_ids": query_ids}


norm_eps = 1e-05

def reference(tokens, acts, resid, cotangent, weight, gain, proj_in, proj_out, tok_weight, lengths, queries, query_ids):
    tok_count = acts.shape[0]
    block_width = FF // N_MP
    act_blocks = acts.reshape(tok_count, N_MP, block_width).transpose(1, 0, 2)
    weight_blocks = weight.reshape(N_MP, block_width, D)

    def add_block(running, shard_pair):
        shard_term = jnp.dot(shard_pair[0], shard_pair[1], preferred_element_type=jnp.float32)
        shard_term = lax.optimization_barrier(shard_term.astype(jnp.bfloat16)).astype(jnp.float32)
        return (running + shard_term, None)
    layer_out, _ = lax.scan(add_block, jnp.zeros((tok_count, D), jnp.float32), (act_blocks, weight_blocks))
    pre_norm = resid.astype(jnp.float32) + layer_out
    scaled_cot = gain.astype(jnp.float32)[None, :] * cotangent.astype(jnp.float32)
    mean_sq = lax.optimization_barrier(jnp.mean(pre_norm * pre_norm, axis=1, keepdims=True))
    mean_cross = lax.optimization_barrier(jnp.mean(pre_norm * scaled_cot, axis=1, keepdims=True))
    rstd = lax.rsqrt(mean_sq + norm_eps)
    out_grad = (rstd * (scaled_cot - pre_norm * rstd * rstd * mean_cross)).astype(jnp.bfloat16)
    in_sk = jnp.dot(acts, proj_in, preferred_element_type=jnp.float32)
    out_sk = jnp.dot(out_grad, proj_out, preferred_element_type=jnp.float32)
    alive_mask = jnp.arange(SEQ, dtype=jnp.int32)[None, :] < lengths[:, None]
    tok_scale = jnp.where(alive_mask, tok_weight[tokens], jnp.float32(0.0)) / jnp.sqrt(jnp.float32(SEQ))
    doc_count = tokens.shape[0]
    in_weighted = in_sk.reshape(doc_count, SEQ, R) * tok_scale[:, :, None]
    out_rows = out_sk.reshape(doc_count, SEQ, R)
    sketch = jnp.einsum('dtr,dts->drs', in_weighted, out_rows, precision=lax.Precision.HIGHEST)
    sketch = sketch.reshape(doc_count, R * R).astype(jnp.bfloat16)
    per_query = lax.dot_general(sketch, queries, (((1,), (1,)), ((), ())), preferred_element_type=jnp.float32)
    group_table = (query_ids[:, None] == jnp.arange(QG, dtype=jnp.int32)[None, :]).astype(jnp.float32)
    scores = jnp.dot(per_query, group_table, precision=lax.Precision.HIGHEST)
    return (pre_norm.astype(jnp.bfloat16), scores)
```

```python
import jax
import jax.numpy as jnp
from jax import lax
from jax.sharding import PartitionSpec as P

QG = 256
CHUNKS = 4


norm_eps = 1e-05


def split_dot(values, proj):
    high = values.astype(jnp.bfloat16)
    low = (values - high.astype(jnp.float32)).astype(jnp.bfloat16)
    both = jnp.dot(
        jnp.concatenate([high, low], axis=0), proj, preferred_element_type=jnp.float32
    )
    rows = values.shape[0]
    return both[:rows] + both[rows:]


def group_sums(queries, own_ids, group_count):
    table = (jnp.arange(group_count, dtype=jnp.int32)[:, None] == own_ids[None, :]).astype(
        jnp.bfloat16
    )
    return jnp.dot(table, queries, preferred_element_type=jnp.float32)


def score_tail(
    in_and_cot, pre_side, tok_scale, grouped, seq_len, doc_count, sketch_rank, width_full
):
    rows = in_and_cot.shape[0]
    in_sk = in_and_cot[:, :sketch_rank]
    cot_sk = in_and_cot[:, sketch_rank:]
    pre_sk = pre_side[:, :sketch_rank]
    mean_sq = pre_side[:, sketch_rank : sketch_rank + 1] / width_full
    mean_cross = pre_side[:, sketch_rank + 1 : sketch_rank + 2] / width_full
    rstd = lax.rsqrt(mean_sq + norm_eps)
    out_sk = rstd * (cot_sk - pre_sk * (rstd * rstd * mean_cross))
    first = lax.axis_index("mp") * rows
    own_doc = (first + jnp.arange(rows, dtype=jnp.int32)) // seq_len
    own_scale = lax.dynamic_slice_in_dim(tok_scale, first, rows, 0)
    by_doc = jnp.where(
        own_doc[None, :] == jnp.arange(doc_count, dtype=jnp.int32)[:, None],
        own_scale[None, :],
        jnp.float32(0.0),
    )
    weighted = by_doc[:, :, None] * in_sk[None, :, :]
    sketch = jnp.einsum("dtr,ts->drs", weighted, out_sk, precision=lax.Precision.HIGHEST)
    sketch = sketch.reshape(doc_count, sketch_rank * sketch_rank)
    sketch = lax.psum_scatter(sketch, "mp", scatter_dimension=1, tiled=True)
    sketch = sketch.astype(jnp.bfloat16)
    high, low = grouped
    contract = (((1,), (1,)), ((), ()))
    local = lax.dot_general(
        sketch, high, contract, preferred_element_type=jnp.float32
    ) + lax.dot_general(sketch, low, contract, preferred_element_type=jnp.float32)
    return lax.psum(local, "mp")


def per_device(
    tokens,
    acts,
    resid,
    cotangent,
    weight,
    gain,
    proj_in,
    proj_out,
    tok_weight,
    lengths,
    queries,
    query_ids,
):
    doc_count, seq_len = tokens.shape
    tok_count = acts.shape[0]
    sketch_rank = proj_in.shape[1]
    width_full = resid.shape[1] * lax.axis_size("mp")
    rows = tok_count // CHUNKS

    query_rows = queries.shape[0]
    own_ids = lax.dynamic_slice_in_dim(query_ids, lax.axis_index("dp") * query_rows, query_rows, 0)

    alive_mask = jnp.arange(seq_len, dtype=jnp.int32)[None, :] < lengths[:, None]
    tok_scale = jnp.where(alive_mask, tok_weight[tokens], jnp.float32(0.0)) / jnp.sqrt(
        jnp.float32(seq_len)
    )
    tok_scale = tok_scale.reshape(tok_count)

    streams, sides = [], []
    cots = []
    for c in range(CHUNKS):
        part = slice(c * rows, (c + 1) * rows)
        partial = jnp.dot(acts[part], weight, preferred_element_type=jnp.float32)
        layer_out = lax.psum_scatter(
            partial.astype(jnp.bfloat16), "mp", scatter_dimension=1, tiled=True
        ).astype(jnp.float32)
        pre_norm = resid[part].astype(jnp.float32) + layer_out
        scaled_cot = gain.astype(jnp.float32)[None, :] * cotangent[part].astype(jnp.float32)
        cots.append(split_dot(scaled_cot, proj_out))
        sides.append(
            jnp.concatenate(
                [
                    split_dot(pre_norm, proj_out),
                    jnp.sum(pre_norm * pre_norm, axis=1, keepdims=True),
                    jnp.sum(pre_norm * scaled_cot, axis=1, keepdims=True),
                ],
                axis=1,
            )
        )
        streams.append(pre_norm.astype(jnp.bfloat16))
    grouped = lax.psum(group_sums(queries, own_ids, QG), "dp")
    high = grouped.astype(jnp.bfloat16)
    low = (grouped - high.astype(jnp.float32)).astype(jnp.bfloat16)
    in_partial = jnp.dot(acts, proj_in, preferred_element_type=jnp.float32)
    in_and_cot = lax.psum_scatter(
        jnp.concatenate([in_partial, jnp.concatenate(cots, axis=0)], axis=1),
        "mp",
        scatter_dimension=0,
        tiled=True,
    )
    pre_side = lax.psum_scatter(
        jnp.concatenate(sides, axis=0), "mp", scatter_dimension=0, tiled=True
    )
    scores = score_tail(
        in_and_cot,
        pre_side,
        tok_scale,
        (high, low),
        seq_len,
        doc_count,
        sketch_rank,
        width_full,
    )
    return (jnp.concatenate(streams, axis=0), scores)


def solution(mesh):
    placed = (
        P(("groups", "dp"), None),
        P(("groups", "dp"), "mp"),
        P(("groups", "dp"), "mp"),
        P(("groups", "dp"), "mp"),
        P("mp", None),
        P("mp"),
        P("mp", None),
        P("mp", None),
        P(),
        P(("groups", "dp")),
        P("dp", "mp"),
        P(),
    )
    return jax.shard_map(
        per_device,
        mesh=mesh,
        in_specs=placed,
        out_specs=(P(("groups", "dp"), "mp"), P(("groups", "dp"), None)),
        check_vma=False,
    )
```

```python
import functools

import jax
import jax.numpy as jnp
from jax import lax
from jax.experimental import pallas as pl
from jax.experimental.pallas import tpu as pltpu
from jax.sharding import PartitionSpec as P

QG = 256
LANES = 128
TILE = 256
ROWS = 256
DOT_ROWS = 512
WSLOTS = 3
MESH = pl.DeviceIdType.MESH


norm_eps = 1e-05


def split(values):
    high = values.astype(jnp.bfloat16)
    return high, (values - high.astype(jnp.float32)).astype(jnp.bfloat16)


def split_dot(values, proj):
    high, low = split(values)
    return jnp.dot(high, proj, preferred_element_type=jnp.float32) + jnp.dot(
        low, proj, preferred_element_type=jnp.float32
    )


def group_sums(queries, own_ids, group_count):
    table = (jnp.arange(group_count, dtype=jnp.int32)[:, None] == own_ids[None, :]).astype(
        jnp.bfloat16
    )
    return jnp.dot(table, queries, preferred_element_type=jnp.float32)


def kernel(
    n,
    rank,
    acts_hbm,
    weight_hbm,
    resid_hbm,
    cot_hbm,
    gain_ref,
    proj_in_ref,
    proj_out_ref,
    scale_ref,
    stream_hbm,
    sketch_ref,
    acts,
    resid,
    cot,
    tiles,
    ring,
    acc,
    cot_side,
    pre_side,
    cot_parts,
    pre_parts,
    sk_own,
    sk_parts,
    load_sems,
    tile_sems,
    ring_send,
    ring_recv,
    out_sems,
    cot_send,
    cot_recv,
    pre_send,
    pre_recv,
    sk_send,
    sk_recv,
):
    me = lax.axis_index("mp")
    right = lax.rem(me + 1, n)
    tok_count = acts.shape[0]
    block = resid.shape[1]
    tile = acc.shape[1]
    subs = block // tile
    total = n * subs
    own_rows = tok_count // n
    width_full = block * n
    row_blk = min(ROWS, tok_count)
    dot_blk = min(DOT_ROWS, tok_count)

    loads = [
        pltpu.make_async_copy(src, dst, load_sems.at[i])
        for i, (src, dst) in enumerate(((acts_hbm, acts), (cot_hbm, cot), (resid_hbm, resid)))
    ]

    def tile_copy(t):
        owner = lax.rem(me - 1 - t // subs + 2 * n, n)
        at = pl.multiple_of(owner * block + lax.rem(t, subs) * tile, tile)
        slot = lax.rem(t, WSLOTS)
        return pltpu.make_async_copy(
            weight_hbm.at[:, pl.ds(at, tile)], tiles.at[slot], tile_sems.at[slot]
        )

    def hop(t):
        return pltpu.make_async_remote_copy(
            src_ref=ring.at[t],
            dst_ref=ring.at[t + subs],
            send_sem=ring_send.at[t],
            recv_sem=ring_recv.at[t + subs],
            device_id={"mp": right},
            device_id_type=MESH,
        )

    def out_copy(j):
        at = pl.multiple_of(j * tile, tile)
        return pltpu.make_async_copy(
            ring.at[total - subs + j], stream_hbm.at[:, pl.ds(at, tile)], out_sems.at[j]
        )

    def spread(source, parts, send, recv, whole):
        copies = []
        for k in range(1, n):
            peer = lax.rem(me + k, n)
            src = source
            if not whole:
                src = source.at[pl.ds(pl.multiple_of(peer * own_rows, own_rows), own_rows)]
            copies.append(
                pltpu.make_async_remote_copy(
                    src_ref=src,
                    dst_ref=parts.at[k - 1],
                    send_sem=send.at[k - 1],
                    recv_sem=recv.at[k - 1],
                    device_id={"mp": peer},
                    device_id_type=MESH,
                )
            )
        return copies

    tile_copy(0).start()
    loads[0].start()
    tile_copy(1).start()
    loads[1].start()
    loads[2].start()

    barrier = pltpu.get_barrier_semaphore()
    for k in range(1, n):
        pl.semaphore_signal(
            barrier, inc=1, device_id={"mp": lax.rem(me + k, n)}, device_id_type=MESH
        )
    pl.semaphore_wait(barrier, n - 1)

    cot_side[...] = jnp.zeros_like(cot_side)
    pre_side[...] = jnp.zeros_like(pre_side)
    loads[0].wait()

    lane = lax.broadcasted_iota(jnp.int32, (row_blk, LANES), 1)

    def scaled(rows, cols):
        return gain_ref[0:1, cols].astype(jnp.float32) * cot[rows, cols].astype(jnp.float32)

    def row_loop(size, body):
        def step(b, carry):
            body(pl.ds(pl.multiple_of(b * size, size), size))
            return carry

        lax.fori_loop(0, tok_count // size, step, 0)

    cot_copies = spread(cot_side, cot_parts, cot_send, cot_recv, False)

    def one(t, carry):
        @pl.when(t + 2 < total)
        def _():
            tile_copy(t + 2).start()

        tile_copy(t).wait()
        slot = lax.rem(t, WSLOTS)

        def mul(rows):
            acc[rows, :] = jnp.dot(
                acts[rows, :], tiles[slot], preferred_element_type=jnp.float32
            )

        row_loop(dot_blk, mul)
        j = lax.rem(t, subs)
        cols = pl.ds(pl.multiple_of(j * tile, tile), tile)

        @pl.when(t < subs)
        def _():
            def put(rows):
                ring[t, rows, :] = acc[rows, :].astype(jnp.bfloat16)

            row_loop(row_blk, put)
            hop(t).start()

            @pl.when(t == 0)
            def _():
                loads[1].wait()
                loads[2].wait()

            def side(rows):
                cot_side[rows, :] += split_dot(scaled(rows, cols), proj_out_ref[cols, :])

            row_loop(row_blk, side)

            @pl.when(t == subs - 1)
            def _():
                def ins(rows):
                    cot_side[rows, :] += jnp.dot(
                        acts[rows, :], proj_in_ref[...], preferred_element_type=jnp.float32
                    )

                row_loop(row_blk, ins)
                for copy in cot_copies:
                    copy.start()

        @pl.when(t >= subs)
        def _():
            hop(t - subs).wait_recv()

        @pl.when(jnp.logical_and(t >= subs, t < total - subs))
        def _():
            def add(rows):
                ring[t, rows, :] = (acc[rows, :] + ring[t, rows, :].astype(jnp.float32)).astype(
                    jnp.bfloat16
                )

            row_loop(row_blk, add)
            hop(t).start()

        @pl.when(t >= total - subs)
        def _():
            def last(rows):
                pre = resid[rows, cols].astype(jnp.float32) + (
                    acc[rows, :] + ring[t, rows, :].astype(jnp.float32)
                )
                ring[t, rows, :] = pre.astype(jnp.bfloat16)
                squares = jnp.sum(pre * pre, axis=1, keepdims=True)
                crosses = jnp.sum(pre * scaled(rows, cols), axis=1, keepdims=True)
                extra = jnp.where(
                    lane == rank, squares, jnp.where(lane == rank + 1, crosses, jnp.float32(0.0))
                )
                pre_side[rows, :] += split_dot(pre, proj_out_ref[cols, :]) + extra

            row_loop(row_blk, last)
            out_copy(j).start()

        return carry

    lax.fori_loop(0, total, one, 0)

    pre_copies = spread(pre_side, pre_parts, pre_send, pre_recv, False)
    for copy in pre_copies:
        copy.start()
    mine = pl.ds(pl.multiple_of(me * own_rows, own_rows), own_rows)
    cots = cot_side[mine, :]
    for k in range(1, n):
        cot_copies[k - 1].wait_recv()
        cots += cot_parts[k - 1]
    pres = pre_side[mine, :]
    for k in range(1, n):
        pre_copies[k - 1].wait_recv()
        pres += pre_parts[k - 1]
    rstd = lax.rsqrt(pres[:, rank : rank + 1] / width_full + norm_eps)
    factor = rstd * rstd * (pres[:, rank + 1 : rank + 2] / width_full)
    own_lane = lax.broadcasted_iota(jnp.int32, (own_rows, LANES), 1)
    outs = jnp.where(own_lane < rank, rstd * (cots - pres * factor), jnp.float32(0.0))
    for d in range(scale_ref.shape[1]):
        full = lax.dot_general(
            cots,
            outs * scale_ref[:, d : d + 1],
            (((0,), (0,)), ((), ())),
            preferred_element_type=jnp.float32,
            precision=lax.Precision.HIGHEST,
        )
        sk_own[d] = full[LANES - rank :, :]
    sk_copies = spread(sk_own, sk_parts, sk_send, sk_recv, True)
    for copy in sk_copies:
        copy.start()
    sums = sk_own[...]
    for k in range(1, n):
        sk_copies[k - 1].wait_recv()
        sums += sk_parts[k - 1]
    sketch_ref[...] = sums

    def drain(t, carry):
        hop(t).wait_send()
        return carry

    lax.fori_loop(0, total - subs, drain, 0)

    def drain_out(j, carry):
        out_copy(j).wait()
        return carry

    lax.fori_loop(0, subs, drain_out, 0)
    for copy in cot_copies + pre_copies + sk_copies:
        copy.wait_send()


def per_device(
    tokens,
    acts,
    resid,
    cotangent,
    weight,
    gain,
    proj_in,
    proj_out,
    tok_weight,
    lengths,
    queries,
    query_ids,
):
    doc_count, seq_len = tokens.shape
    tok_count, depth = acts.shape
    rank = proj_in.shape[1]
    block = resid.shape[1]
    feat_count = queries.shape[1]
    n = lax.axis_size("mp")
    me = lax.axis_index("mp")
    tile = min(TILE, block)
    subs = block // tile
    own_rows = tok_count // n

    query_rows = queries.shape[0]
    own_ids = lax.dynamic_slice_in_dim(query_ids, lax.axis_index("dp") * query_rows, query_rows, 0)
    grouped = lax.psum(group_sums(queries, own_ids, QG), "dp")

    place = me * own_rows + jnp.arange(own_rows, dtype=jnp.int32)
    own_tokens = lax.dynamic_slice_in_dim(tokens.reshape(tok_count), me * own_rows, own_rows, 0)
    docs = jnp.arange(doc_count, dtype=jnp.int32)[None, :]
    alive = jnp.logical_and(
        (place // seq_len)[:, None] == docs, (place % seq_len)[:, None] < lengths[None, :]
    )
    scale = jnp.where(alive, tok_weight[own_tokens][:, None], jnp.float32(0.0)) / jnp.sqrt(
        jnp.float32(seq_len)
    )

    bf16, f32 = jnp.bfloat16, jnp.float32
    any_space = pl.BlockSpec(memory_space=pl.ANY)
    vmem = pl.BlockSpec(memory_space=pltpu.VMEM)
    dma = pltpu.SemaphoreType.DMA
    stream, sketch = pl.pallas_call(
        functools.partial(kernel, n, rank),
        out_shape=(
            jax.ShapeDtypeStruct((tok_count, block), bf16),
            jax.ShapeDtypeStruct((doc_count, rank, LANES), f32),
        ),
        in_specs=[any_space] * 4 + [vmem] * 4,
        out_specs=(any_space, vmem),
        scratch_shapes=[
            pltpu.VMEM((tok_count, depth), bf16),
            pltpu.VMEM((tok_count, block), bf16),
            pltpu.VMEM((tok_count, block), bf16),
            pltpu.VMEM((WSLOTS, depth, tile), bf16),
            pltpu.VMEM((n * subs, tok_count, tile), bf16),
            pltpu.VMEM((tok_count, tile), f32),
            pltpu.VMEM((tok_count, LANES), f32),
            pltpu.VMEM((tok_count, LANES), f32),
            pltpu.VMEM((n - 1, own_rows, LANES), f32),
            pltpu.VMEM((n - 1, own_rows, LANES), f32),
            pltpu.VMEM((doc_count, rank, LANES), f32),
            pltpu.VMEM((n - 1, doc_count, rank, LANES), f32),
            dma((3,)),
            dma((WSLOTS,)),
            dma((n * subs,)),
            dma((n * subs,)),
            dma((subs,)),
        ]
        + [dma((n - 1,))] * 6,
        compiler_params=pltpu.CompilerParams(
            collective_id=0, has_side_effects=True, vmem_limit_bytes=60 * 1024 * 1024
        ),
        cost_estimate=pl.CostEstimate(
            flops=2 * tok_count * depth * block * n,
            bytes_accessed=2 * depth * block * n,
            transcendentals=0,
        ),
    )(
        acts,
        weight,
        resid,
        cotangent,
        gain.reshape(1, block),
        jnp.pad(proj_in, ((0, 0), (LANES - rank, 0))),
        jnp.pad(proj_out, ((0, 0), (0, LANES - rank))),
        scale,
    )

    sketch = sketch[:, :, :rank].reshape(doc_count, rank * rank).astype(bf16)
    sketch = lax.dynamic_slice_in_dim(sketch, me * feat_count, feat_count, 1)
    high, low = split(grouped)
    contract = (((1,), (1,)), ((), ()))
    local = lax.dot_general(
        sketch, high, contract, preferred_element_type=f32
    ) + lax.dot_general(sketch, low, contract, preferred_element_type=f32)
    return (stream, lax.psum(local, "mp"))


def solution(mesh):
    placed = (
        P(("groups", "dp"), None),
        P(("groups", "dp"), "mp"),
        P(("groups", "dp"), "mp"),
        P(("groups", "dp"), "mp"),
        P("mp", None),
        P("mp"),
        P("mp", None),
        P("mp", None),
        P(),
        P(("groups", "dp")),
        P("dp", "mp"),
        P(),
    )
    return jax.shard_map(
        per_device,
        mesh=mesh,
        in_specs=placed,
        out_specs=(P(("groups", "dp"), "mp"), P(("groups", "dp"), None)),
        check_vma=False,
    )
```

```python
import functools

import jax
import jax.numpy as jnp
from jax import lax
from jax.experimental import pallas as pl
from jax.experimental.pallas import tpu as pltpu
from jax.sharding import PartitionSpec as P

QG = 256
LANES = 128
TILE = 256
ROWS = 256
DOT_ROWS = 512
WSLOTS = 3
MESH = pl.DeviceIdType.MESH


norm_eps = 1e-05


def split(values):
    high = values.astype(jnp.bfloat16)
    return high, (values - high.astype(jnp.float32)).astype(jnp.bfloat16)


def dot_t(left, right):
    return lax.dot_general(
        left, right, (((1,), (1,)), ((), ())), preferred_element_type=jnp.float32
    )


def split_dot(values, proj):
    high, low = split(values)
    return dot_t(high, proj) + dot_t(low, proj)


def group_sums(queries, own_ids, group_count):
    table = (jnp.arange(group_count, dtype=jnp.int32)[:, None] == own_ids[None, :]).astype(
        jnp.bfloat16
    )
    return jnp.dot(table, queries, preferred_element_type=jnp.float32)


def kernel(
    n,
    rank,
    acts_hbm,
    weight_hbm,
    resid_hbm,
    cot_hbm,
    gain_ref,
    proj_in_ref,
    proj_out_ref,
    scale_ref,
    stream_hbm,
    sketch_ref,
    acts,
    resid,
    cot,
    tiles,
    ring,
    acc,
    cot_side,
    pre_side,
    wide_in,
    wide_out,
    stats,
    stat_parts,
    flat,
    both,
    both_parts,
    sk_own,
    sk_parts,
    load_sems,
    tile_sems,
    ring_send,
    ring_recv,
    out_sems,
    stat_send,
    stat_recv,
    both_send,
    both_recv,
    sk_send,
    sk_recv,
):
    me = lax.axis_index("mp")
    right = lax.rem(me + 1, n)
    tok_count = acts.shape[0]
    block = resid.shape[1]
    tile = acc.shape[1]
    subs = block // tile
    total = n * subs
    own_rows = tok_count // n
    width_full = block * n
    row_blk = min(ROWS, tok_count)
    dot_blk = min(DOT_ROWS, tok_count)

    loads = [
        pltpu.make_async_copy(src, dst, load_sems.at[i])
        for i, (src, dst) in enumerate(((acts_hbm, acts), (cot_hbm, cot), (resid_hbm, resid)))
    ]

    def tile_copy(t):
        owner = lax.rem(me - 1 - t // subs + 2 * n, n)
        at = pl.multiple_of(owner * block + lax.rem(t, subs) * tile, tile)
        slot = lax.rem(t, WSLOTS)
        return pltpu.make_async_copy(
            weight_hbm.at[:, pl.ds(at, tile)], tiles.at[slot], tile_sems.at[slot]
        )

    def hop(t):
        return pltpu.make_async_remote_copy(
            src_ref=ring.at[t],
            dst_ref=ring.at[t + subs],
            send_sem=ring_send.at[t],
            recv_sem=ring_recv.at[t + subs],
            device_id={"mp": right},
            device_id_type=MESH,
        )

    def out_copy(j):
        at = pl.multiple_of(j * tile, tile)
        return pltpu.make_async_copy(
            ring.at[total - subs + j], stream_hbm.at[:, pl.ds(at, tile)], out_sems.at[j]
        )

    def spread(source, parts, send, recv, whole):
        copies = []
        for k in range(1, n):
            peer = lax.rem(me + k, n)
            src = source
            if not whole:
                src = source.at[pl.ds(pl.multiple_of(peer * own_rows, own_rows), own_rows)]
            copies.append(
                pltpu.make_async_remote_copy(
                    src_ref=src,
                    dst_ref=parts.at[k - 1],
                    send_sem=send.at[k - 1],
                    recv_sem=recv.at[k - 1],
                    device_id={"mp": peer},
                    device_id_type=MESH,
                )
            )
        return copies

    tile_copy(0).start()
    loads[0].start()
    tile_copy(1).start()
    loads[1].start()
    loads[2].start()

    barrier = pltpu.get_barrier_semaphore()
    for k in range(1, n):
        pl.semaphore_signal(
            barrier, inc=1, device_id={"mp": lax.rem(me + k, n)}, device_id_type=MESH
        )
    pl.semaphore_wait(barrier, n - 1)

    cot_side[...] = jnp.zeros_like(cot_side)
    pre_side[...] = jnp.zeros_like(pre_side)
    wide_in[...] = jnp.zeros_like(wide_in)
    wide_in[LANES - rank :, :] = proj_in_ref[...]
    wide_out[...] = jnp.zeros_like(wide_out)
    wide_out[:rank, :] = proj_out_ref[...]
    loads[0].wait()

    lane = lax.broadcasted_iota(jnp.int32, (row_blk, LANES), 1)

    def scaled(rows, cols):
        return gain_ref[0:1, cols].astype(jnp.float32) * cot[rows, cols].astype(jnp.float32)

    def row_loop(size, body):
        def step(b, carry):
            body(pl.ds(pl.multiple_of(b * size, size), size))
            return carry

        lax.fori_loop(0, tok_count // size, step, 0)

    def one(t, carry):
        @pl.when(t + 2 < total)
        def _():
            tile_copy(t + 2).start()

        tile_copy(t).wait()
        slot = lax.rem(t, WSLOTS)

        def mul(rows):
            acc[rows, :] = jnp.dot(
                acts[rows, :], tiles[slot], preferred_element_type=jnp.float32
            )

        row_loop(dot_blk, mul)
        j = lax.rem(t, subs)
        cols = pl.ds(pl.multiple_of(j * tile, tile), tile)

        @pl.when(t < subs)
        def _():
            def put(rows):
                ring[t, rows, :] = acc[rows, :].astype(jnp.bfloat16)

            row_loop(row_blk, put)
            hop(t).start()

            @pl.when(t == 0)
            def _():
                loads[1].wait()
                loads[2].wait()

            def side(rows):
                cot_side[rows, :] += split_dot(scaled(rows, cols), wide_out[:, cols])

            row_loop(row_blk, side)

            @pl.when(t == subs - 1)
            def _():
                def ins(rows):
                    cot_side[rows, :] += dot_t(acts[rows, :], wide_in[...])

                row_loop(row_blk, ins)

        @pl.when(t >= subs)
        def _():
            hop(t - subs).wait_recv()

        @pl.when(jnp.logical_and(t >= subs, t < total - subs))
        def _():
            def add(rows):
                ring[t, rows, :] = (acc[rows, :] + ring[t, rows, :].astype(jnp.float32)).astype(
                    jnp.bfloat16
                )

            row_loop(row_blk, add)
            hop(t).start()

        @pl.when(t >= total - subs)
        def _():
            def last(rows):
                pre = resid[rows, cols].astype(jnp.float32) + (
                    acc[rows, :] + ring[t, rows, :].astype(jnp.float32)
                )
                ring[t, rows, :] = pre.astype(jnp.bfloat16)
                squares = jnp.sum(pre * pre, axis=1, keepdims=True)
                crosses = jnp.sum(pre * scaled(rows, cols), axis=1, keepdims=True)
                extra = jnp.where(
                    lane == rank, squares, jnp.where(lane == rank + 1, crosses, jnp.float32(0.0))
                )
                pre_side[rows, :] += split_dot(pre, wide_out[:, cols]) + extra

            row_loop(row_blk, last)
            out_copy(j).start()

        return carry

    lax.fori_loop(0, total, one, 0)

    stats[...] = pre_side[...].T[rank : rank + 8, :]
    stat_copies = spread(stats, stat_parts, stat_send, stat_recv, True)
    for copy in stat_copies:
        copy.start()
    flat[...] = jnp.zeros_like(flat)
    sums = stats[...]
    for k in range(1, n):
        stat_copies[k - 1].wait_recv()
        sums += stat_parts[k - 1]
    flat[0:8, :] = sums
    pre_stats = flat[...].T
    rstd = lax.rsqrt(pre_stats[:, 0:1] / width_full + norm_eps)
    factor = rstd * rstd * (pre_stats[:, 1:2] / width_full)
    cots = cot_side[...]
    all_lane = lax.broadcasted_iota(jnp.int32, (tok_count, LANES), 1)
    both[...] = jnp.where(
        all_lane < rank, rstd * (cots - pre_side[...] * factor), cots
    ).astype(jnp.bfloat16)
    both_copies = spread(both, both_parts, both_send, both_recv, False)
    for copy in both_copies:
        copy.start()
    mine = pl.ds(pl.multiple_of(me * own_rows, own_rows), own_rows)
    sides = both[mine, :].astype(jnp.float32)
    for k in range(1, n):
        both_copies[k - 1].wait_recv()
        sides += both_parts[k - 1].astype(jnp.float32)
    own_lane = lax.broadcasted_iota(jnp.int32, (own_rows, LANES), 1)
    outs = jnp.where(own_lane < rank, sides, jnp.float32(0.0))
    for d in range(scale_ref.shape[1]):
        full = lax.dot_general(
            sides,
            outs * scale_ref[:, d : d + 1],
            (((0,), (0,)), ((), ())),
            preferred_element_type=jnp.float32,
            precision=lax.Precision.HIGHEST,
        )
        sk_own[d] = full[LANES - rank :, :]
    sk_copies = spread(sk_own, sk_parts, sk_send, sk_recv, True)
    for copy in sk_copies:
        copy.start()
    sums = sk_own[...]
    for k in range(1, n):
        sk_copies[k - 1].wait_recv()
        sums += sk_parts[k - 1]
    sketch_ref[...] = sums

    def drain(t, carry):
        hop(t).wait_send()
        return carry

    lax.fori_loop(0, total - subs, drain, 0)

    def drain_out(j, carry):
        out_copy(j).wait()
        return carry

    lax.fori_loop(0, subs, drain_out, 0)
    for copy in stat_copies + both_copies + sk_copies:
        copy.wait_send()


def score_kernel(n, sketch_ref, high_ref, low_ref, out_ref, own, parts, send, recv):
    me = lax.axis_index("mp")
    barrier = pltpu.get_barrier_semaphore()
    for k in range(1, n):
        pl.semaphore_signal(
            barrier, inc=1, device_id={"mp": lax.rem(me + k, n)}, device_id_type=MESH
        )
    own[...] = dot_t(sketch_ref[...], high_ref[...]) + dot_t(sketch_ref[...], low_ref[...])
    pl.semaphore_wait(barrier, n - 1)
    copies = [
        pltpu.make_async_remote_copy(
            src_ref=own,
            dst_ref=parts.at[k - 1],
            send_sem=send.at[k - 1],
            recv_sem=recv.at[k - 1],
            device_id={"mp": lax.rem(me + k, n)},
            device_id_type=MESH,
        )
        for k in range(1, n)
    ]
    for copy in copies:
        copy.start()
    sums = own[...]
    for k in range(1, n):
        copies[k - 1].wait_recv()
        sums += parts[k - 1]
    out_ref[...] = sums
    for copy in copies:
        copy.wait_send()


def per_device(
    tokens,
    acts,
    resid,
    cotangent,
    weight,
    gain,
    proj_in,
    proj_out,
    tok_weight,
    lengths,
    queries,
    query_ids,
):
    doc_count, seq_len = tokens.shape
    tok_count, depth = acts.shape
    rank = proj_in.shape[1]
    block = resid.shape[1]
    feat_count = queries.shape[1]
    n = lax.axis_size("mp")
    me = lax.axis_index("mp")
    tile = min(TILE, block)
    subs = block // tile
    own_rows = tok_count // n

    query_rows = queries.shape[0]
    own_ids = lax.dynamic_slice_in_dim(query_ids, lax.axis_index("dp") * query_rows, query_rows, 0)
    grouped = lax.psum(group_sums(queries, own_ids, QG), "dp")

    place = me * own_rows + jnp.arange(own_rows, dtype=jnp.int32)
    own_tokens = lax.dynamic_slice_in_dim(tokens.reshape(tok_count), me * own_rows, own_rows, 0)
    docs = jnp.arange(doc_count, dtype=jnp.int32)[None, :]
    alive = jnp.logical_and(
        (place // seq_len)[:, None] == docs, (place % seq_len)[:, None] < lengths[None, :]
    )
    scale = jnp.where(alive, tok_weight[own_tokens][:, None], jnp.float32(0.0)) / jnp.sqrt(
        jnp.float32(seq_len)
    )

    bf16, f32 = jnp.bfloat16, jnp.float32
    any_space = pl.BlockSpec(memory_space=pl.ANY)
    vmem = pl.BlockSpec(memory_space=pltpu.VMEM)
    dma = pltpu.SemaphoreType.DMA
    stream, sketch = pl.pallas_call(
        functools.partial(kernel, n, rank),
        out_shape=(
            jax.ShapeDtypeStruct((tok_count, block), bf16),
            jax.ShapeDtypeStruct((doc_count, rank, LANES), f32),
        ),
        in_specs=[any_space] * 4 + [vmem] * 4,
        out_specs=(any_space, vmem),
        scratch_shapes=[
            pltpu.VMEM((tok_count, depth), bf16),
            pltpu.VMEM((tok_count, block), bf16),
            pltpu.VMEM((tok_count, block), bf16),
            pltpu.VMEM((WSLOTS, depth, tile), bf16),
            pltpu.VMEM((n * subs, tok_count, tile), bf16),
            pltpu.VMEM((tok_count, tile), f32),
            pltpu.VMEM((tok_count, LANES), f32),
            pltpu.VMEM((tok_count, LANES), f32),
            pltpu.VMEM((LANES, depth), bf16),
            pltpu.VMEM((LANES, block), bf16),
            pltpu.VMEM((8, tok_count), f32),
            pltpu.VMEM((n - 1, 8, tok_count), f32),
            pltpu.VMEM((LANES, tok_count), f32),
            pltpu.VMEM((tok_count, LANES), bf16),
            pltpu.VMEM((n - 1, own_rows, LANES), bf16),
            pltpu.VMEM((doc_count, rank, LANES), f32),
            pltpu.VMEM((n - 1, doc_count, rank, LANES), f32),
            dma((3,)),
            dma((WSLOTS,)),
            dma((n * subs,)),
            dma((n * subs,)),
            dma((subs,)),
        ]
        + [dma((n - 1,))] * 6,
        compiler_params=pltpu.CompilerParams(
            collective_id=0, has_side_effects=True, vmem_limit_bytes=60 * 1024 * 1024
        ),
        cost_estimate=pl.CostEstimate(
            flops=2 * tok_count * depth * block * n,
            bytes_accessed=2 * depth * block * n,
            transcendentals=0,
        ),
    )(
        acts,
        weight,
        resid,
        cotangent,
        gain.reshape(1, block),
        proj_in.T,
        proj_out.T,
        scale,
    )

    sketch = sketch[:, :, :rank].reshape(doc_count, rank * rank).astype(bf16)
    sketch = lax.dynamic_slice_in_dim(sketch, me * feat_count, feat_count, 1)
    high, low = split(grouped)
    scores = pl.pallas_call(
        functools.partial(score_kernel, n),
        out_shape=jax.ShapeDtypeStruct((doc_count, QG), f32),
        in_specs=[vmem] * 3,
        out_specs=vmem,
        scratch_shapes=[
            pltpu.VMEM((doc_count, QG), f32),
            pltpu.VMEM((n - 1, doc_count, QG), f32),
            dma((n - 1,)),
            dma((n - 1,)),
        ],
        compiler_params=pltpu.CompilerParams(
            collective_id=1, has_side_effects=True, vmem_limit_bytes=16 * 1024 * 1024
        ),
    )(sketch, high, low)
    return (stream, scores)


def solution(mesh):
    placed = (
        P(("groups", "dp"), None),
        P(("groups", "dp"), "mp"),
        P(("groups", "dp"), "mp"),
        P(("groups", "dp"), "mp"),
        P("mp", None),
        P("mp"),
        P("mp", None),
        P("mp", None),
        P(),
        P(("groups", "dp")),
        P("dp", "mp"),
        P(),
    )
    return jax.shard_map(
        per_device,
        mesh=mesh,
        in_specs=placed,
        out_specs=(P(("groups", "dp"), "mp"), P(("groups", "dp"), None)),
        check_vma=False,
    )
```
